256 devices in a mesh: rep: 32 (over z_hi, y, core), fsdp: 8 (over x, z_lo).
Axes of the slice: x: 4, y: 4, z: 8 (z_hi: 4, z_lo: 2; z = z_hi * 2 + z_lo), core: 2. Of those that a mesh axis runs over, the one named last changes fastest.
Arguments:
- local_fragment: bfloat16 [32, 2, 8192, 1024], P('rep', None, 'fsdp'), may hold values from -6 to 6
- anchor: float32 [2, 8192, 1024], P(None, ('fsdp', 'rep')), may hold values from -6 to 6
- momentum: float32 [2, 8192, 1024], P(None, ('fsdp', 'rep')), may hold values from -4 to 4
- next_weights: bfloat16 [32, 8192, 1024], P('rep', 'fsdp'), may hold values from -0.0625 to 0.0625
- activations: bfloat16 [65536, 8192], P(('rep', 'fsdp')), may hold values from -6 to 6
- norm_gain: float32 [8192], replicated, may hold values from 0.25 to 1.75
Outputs:
- new_anchor: float32 [2, 8192, 1024], P(None, ('fsdp', 'rep'))
- new_momentum: float32 [2, 8192, 1024], P(None, ('fsdp', 'rep'))
- keys_values: bfloat16 [65536, 1024], P(('rep', 'fsdp'))
The draws below stay inside these ranges and needn't reach their ends.
All inputs are finite; a program needn't handle non-finite values.
Results may differ from the reference program's by a relative error of at most 0.011.
Values may be sent and summed in bfloat16 or wider, within the bound.
No kernel may reach another device: no remote copies, remote signals or barrier semaphores. Data moves between devices by JAX's collectives and lax.ppermute only.
A program may use at most 128 MiB of HBM per device.

```python
import jax
import jax.numpy as jnp
from jax import lax

D = 8192
KVC = 1024
LAYERS = 2
TOK_DEV = 256
TOKENS = 65536
N_REP = 32
N_FSDP = 8


def raised(array, key, source, target, blocks, factor):
    owner, partner = [(jnp.arange(array.shape[axis_at]) // (array.shape[axis_at] // blocks)).reshape([-1 if axis == axis_at else 1 for axis in range(array.ndim)]) for axis_at in (source, target)]
    chosen = jax.random.permutation(key, blocks)[partner]
    strong = (owner == chosen) | (owner == (partner + blocks // 2) % blocks)
    return jnp.where(strong, factor * array, array)


def level_of(own_key, extent, cuts, smallest, largest):
    loudness, own = 1.0, jax.random.fold_in(own_key, 6)
    for dim, parts in cuts:
        steps = jnp.exp(jax.random.uniform(jax.random.fold_in(own, dim), (parts,), jnp.float32, smallest / len(cuts), largest / len(cuts)))
        loudness = loudness * jnp.repeat(steps, extent[dim] // parts).reshape([-1 if axis == dim else 1 for axis in range(len(extent))])
    return loudness


def bell_draw(rng, dims, scale, most, cuts=(), kind=jnp.bfloat16):
    result = jax.random.normal(rng, dims, jnp.float32) * scale
    if len(cuts) > 0:
        result = level_of(rng, dims, cuts, -0.22, 0.18) * result
    return jnp.clip(result, min=-most, max=most).astype(kind)


def bell_draw_with(own_key, dims, spread, most, split, heavy, held_as=jnp.bfloat16):
    result = spread * jax.random.normal(own_key, dims, jnp.float32)
    if split:
        result = result * level_of(own_key, dims, split, -0.22, 0.18)
    return jnp.clip(raised(result, jax.random.fold_in(own_key, 3), *heavy), -most, most).astype(held_as)


def setup_inputs(seed: int = 0) -> dict:
    key_list = jax.random.split(jax.random.key(seed), 7)
    local_fragment = bell_draw_with(key_list[0], (N_REP, LAYERS, D, KVC), 1.0, 6.0, ((0, 32), (2, 8)), (0, 2, 32, 2.75))
    anchor = bell_draw(key_list[1], (LAYERS, D, KVC), 1.0, 6.0, ((1, 256),), jnp.float32)
    momentum = bell_draw(key_list[2], (LAYERS, D, KVC), 0.5, 4.0, ((1, 256),), jnp.float32)
    next_weights = bell_draw(key_list[3], (N_REP, D, KVC), D ** -0.5, 0.0625, ((0, 32), (1, 8)))
    activations = bell_draw(key_list[4], (TOKENS, D), 1.0, 6.0, ((0, 256),))
    norm_gain = jnp.clip(1.0 + 0.15 * jax.random.normal(key_list[5], (D,), jnp.float32), 0.25, 1.75)
    return {"local_fragment": local_fragment, "anchor": anchor, "momentum": momentum, "next_weights": next_weights, "activations": activations, "norm_gain": norm_gain}


def reference(local_fragment, anchor, momentum, next_weights, activations, norm_gain):

    def accumulate(carry, replica):
        return (carry + replica.astype(jnp.float32), None)
    total, unused = lax.scan(accumulate, jnp.zeros(anchor.shape, jnp.float32), local_fragment)
    pseudo = anchor - total / N_REP
    new_momentum = 0.9 * momentum + pseudo
    new_anchor = anchor - 0.7 * (pseudo + 0.9 * new_momentum)
    wide = activations.astype(jnp.float32)
    square_mean = lax.optimization_barrier(jnp.mean(wide * wide, axis=-1, keepdims=True))
    normed = (wide * lax.rsqrt(square_mean + 1e-05) * norm_gain).astype(jnp.bfloat16)
    grouped = normed.reshape(N_REP, TOK_DEV * N_FSDP, D)

    def project(pair):
        return jnp.dot(pair[0], pair[1], preferred_element_type=jnp.float32).astype(jnp.bfloat16)
    keys_values = lax.map(project, (grouped, next_weights)).reshape(N_REP * N_FSDP * TOK_DEV, KVC)
    return (new_anchor, new_momentum, keys_values)
```

```python
import jax
import jax.numpy as jnp
from jax import lax
from jax.sharding import PartitionSpec as P

F32, BF16 = jnp.float32, jnp.bfloat16
EPS = 1e-05


def along(sizes, axis, shift):
    pairs = []
    total = 1
    for size in sizes:
        total *= size
    stride = 1
    for size in sizes[axis + 1 :]:
        stride *= size
    for index in range(total):
        at = index // stride % sizes[axis]
        pairs.append((index, index + ((at + shift) % sizes[axis] - at) * stride))
    return pairs


REP = (4, 4, 2)
FSDP = (4, 2)


def move(value, mesh_axis, sizes, axis, shift):
    return lax.ppermute(value, mesh_axis, along(sizes, axis, shift))


def shards(local_fragment, anchor, momentum, next_weights, activations, norm_gain):
    replicas = lax.axis_size("rep")
    rep, fsdp = lax.axis_index("rep"), lax.axis_index("fsdp")
    z_hi, y, core = rep // 8, rep // 2 % 4, rep % 2
    x, z_lo = fsdp // 2, fsdp % 2

    mine = next_weights[0]
    rows = mine.shape[0]
    other = move(mine, "fsdp", FSDP, 1, 1)

    def block(shift):
        owner = (x + shift) % 4
        parts = []
        for which in (z_lo, 1 - z_lo):
            at = (owner * 2 + which) * rows
            a = lax.dynamic_slice_in_dim(activations, at, rows, 1).astype(F32)
            g = lax.dynamic_slice_in_dim(norm_gain, at, rows, 0)
            parts.append((a * g).astype(BF16))
        return jnp.concatenate(parts, 1)

    sent2 = move(block(2), "fsdp", FSDP, 0, 2)
    sent_p = move(block(1), "fsdp", FSDP, 0, 1)
    sent_m = move(block(3), "fsdp", FSDP, 0, 3)
    own = block(0)

    frag = local_fragment[0].reshape(2, 4, 4, 2, 32, 1024)
    pick = lambda a, i, d: lax.dynamic_index_in_dim(a, i, d, keepdims=False)
    got = move(pick(frag, 1 - core, 3), "rep", REP, 2, 1)
    pair = (pick(frag, core, 3).astype(F32) + got.astype(F32)).astype(BF16)
    ys = [move(pick(pair, (y + s) % 4, 2), "rep", REP, 1, s) for s in (1, 2, 3)]
    line = pick(pair, y, 2).astype(F32)
    for part in ys:
        line = line + part.astype(F32)
    line = line.astype(BF16)
    zs = [move(pick(line, (z_hi + s) % 4, 1), "rep", REP, 0, s) for s in (1, 2, 3)]
    total = pick(line, z_hi, 1).astype(F32)
    for part in zs:
        total = total + part.astype(F32)
    pseudo = anchor - total / replicas
    new_momentum = 0.9 * momentum + pseudo
    new_anchor = anchor - 0.7 * (pseudo + 0.9 * new_momentum)

    wide = activations.astype(F32)
    scale = lax.rsqrt(jnp.mean(wide * wide, axis=-1, keepdims=True) + EPS)

    def partial(a):
        return jnp.dot(a[:, :rows], mine, preferred_element_type=F32) + jnp.dot(
            a[:, rows:], other, preferred_element_type=F32
        )

    half = 512
    p2 = partial(sent2).astype(BF16)
    via_p = move(p2[:, :half], "fsdp", FSDP, 0, 1)
    via_m = move(p2[:, half:], "fsdp", FSDP, 0, 3)
    back_m, back_p = partial(sent_p), partial(sent_m)
    to_p = jnp.concatenate([back_p[:, :half] + via_p.astype(F32), back_p[:, half:]], 1).astype(BF16)
    to_m = jnp.concatenate([back_m[:, :half], back_m[:, half:] + via_m.astype(F32)], 1).astype(BF16)
    got_p = move(to_p, "fsdp", FSDP, 0, 1)
    got_m = move(to_m, "fsdp", FSDP, 0, 3)
    projected = partial(own) + got_p.astype(F32) + got_m.astype(F32)
    return (new_anchor, new_momentum, (projected * scale).astype(BF16))


def solution(mesh):
    placed = (
        P("rep", None, "fsdp", None),
        P(None, ("fsdp", "rep"), None),
        P(None, ("fsdp", "rep"), None),
        P("rep", "fsdp", None),
        P(("rep", "fsdp"), None),
        P(),
    )
    return jax.shard_map(
        shards,
        mesh=mesh,
        in_specs=placed,
        out_specs=(
            P(None, ("fsdp", "rep"), None),
            P(None, ("fsdp", "rep"), None),
            P(("rep", "fsdp"), None),
        ),
        check_vma=False,
    )
```

```python
import functools

import jax
import jax.numpy as jnp
from jax import lax
from jax.experimental import pallas as pl
from jax.experimental.pallas import tpu as pltpu
from jax.sharding import PartitionSpec as P

F32, BF16 = jnp.float32, jnp.bfloat16
EPS = 1e-05
REP = (4, 4, 2)
FSDP = (4, 2)
MIB = 1 << 20
PARAMS = pltpu.CompilerParams(vmem_limit_bytes=20 * MIB)
ANY = pl.BlockSpec(memory_space=pl.ANY)
VMEM = pl.BlockSpec(memory_space=pltpu.VMEM)


def move(value, mesh_axis, sizes, axis, shift):
    total, stride = 1, 1
    for size in sizes:
        total *= size
    for size in sizes[axis + 1 :]:
        stride *= size
    pairs = []
    for index in range(total):
        at = index // stride % sizes[axis]
        pairs.append((index, index + ((at + shift) % sizes[axis] - at) * stride))
    return lax.ppermute(value, mesh_axis, pairs)


SLOW = 1 << 28
HBM = pl.BlockSpec(memory_space=pltpu.HBM)
DMA = pltpu.SemaphoreType.DMA


def like(shape, dtype):
    return jax.ShapeDtypeStruct(shape, dtype)


def x_of():
    return lax.axis_index("fsdp") // 2


def z_lo_of():
    return lax.axis_index("fsdp") % 2


def z_hi_of():
    return lax.axis_index("rep") // 8


def y_of():
    return lax.axis_index("rep") // 2 % 4


def core_of():
    return lax.axis_index("rep") % 2


def z_pairs(partner):
    return [(i, partner(i // 8) * 8 + i % 8) for i in range(32)]


def call(kernel, out_shape, flops=0, **rest):
    cost = pl.CostEstimate(flops=flops, bytes_accessed=0, transcendentals=0)
    return pl.pallas_call(
        kernel, out_shape=out_shape, compiler_params=PARAMS, cost_estimate=cost, **rest
    )


def in_hbm(array):
    return pltpu.with_memory_space_constraint(array, pltpu.HBM)


def gained(activations, norm_gain, shifts, after):
    rows, step, n = activations.shape[0], 1024, 2 * len(shifts)

    def kernel(a_ref, g_ref, after_ref, *refs):
        outs, (a_buf, sems), g_bufs = refs[: n // 2], refs[n // 2 : n // 2 + 2], refs[n // 2 + 2 :]
        copies = []
        for k in range(n):
            place = (x_of() + shifts[k // 2]) % 4 * 2 + (z_lo_of() + k % 2) % 2
            at = pl.ds(pl.multiple_of(place * step, step), step)
            copies.append(
                (
                    pltpu.make_async_copy(g_ref.at[at], g_bufs[k], sems.at[2 * k]),
                    pltpu.make_async_copy(a_ref.at[:, at], a_buf.at[k], sems.at[2 * k + 1]),
                )
            )
            for copy in copies[-1]:
                copy.start()
        for k in range(n):
            for copy in copies[k]:
                copy.wait()
            value = a_buf[k].astype(F32) * g_bufs[k][...].reshape(1, step)
            outs[k // 2][:, k % 2 * step : (k % 2 + 1) * step] = value.astype(BF16)

    return call(
        kernel,
        [like((rows, 2 * step), BF16)] * (n // 2),
        in_specs=[HBM, HBM, ANY],
        out_specs=[VMEM] * (n // 2),
        scratch_shapes=[pltpu.VMEM((n, rows, step), BF16), DMA((2 * n,))]
        + [pltpu.VMEM((step,), F32)] * n,
    )(in_hbm(activations), in_hbm(norm_gain), after)


def row_scale(activations, after):
    rows, width = activations.shape
    tile = 64

    def kernel(a_ref, after_ref, out_ref):
        wide = a_ref[...].astype(F32)
        out_ref[...] = lax.rsqrt(jnp.mean(wide * wide, axis=-1, keepdims=True) + EPS)

    return call(
        kernel,
        like((rows, 1), F32),
        grid=(rows // tile,),
        in_specs=[pl.BlockSpec((tile, width), lambda i: (i, 0)), ANY],
        out_specs=pl.BlockSpec((tile, 1), lambda i: (i, 0)),
    )(activations, after)


def pair_sum(mine, got, shift, after):
    shape = (2, 4, 4, 2, 32, 1024)

    def kernel(a_ref, b_ref, after_ref, out_ref):
        total = a_ref[...].astype(F32) + b_ref[...].astype(F32)
        out_ref[...] = total.astype(BF16).reshape(out_ref.shape)

    block = pl.BlockSpec(
        (1, 4, 1, 1, 32, 1024), lambda i: (i, 0, (y_of() + shift) % 4, core_of(), 0, 0)
    )
    return call(
        kernel,
        like((2, 4, 32, 1024), BF16),
        grid=(2,),
        in_specs=[block, block, ANY],
        out_specs=pl.BlockSpec((1, 4, 32, 1024), lambda i: (i, 0, 0, 0)),
    )(mine.reshape(shape), got.reshape(shape), after)


def line_sum(parts, after):
    def kernel(a, b, c, d, after_ref, send_ref, keep_ref):
        z_hi = z_hi_of()
        near = z_hi + 1 - 2 * (z_hi % 2)
        for ref, owner in ((send_ref, near), (keep_ref, z_hi)):
            for i, at in enumerate((owner, 3 - owner)):
                total = a[:, at].astype(F32) + b[:, at].astype(F32)
                total = total + c[:, at].astype(F32) + d[:, at].astype(F32)
                ref[i] = total.astype(BF16)

    return call(
        kernel,
        [like((2, 2, 32, 1024), BF16)] * 2,
        in_specs=[VMEM] * 4 + [ANY],
        out_specs=[VMEM] * 2,
    )(*parts, after)


def halves_sum(keep, got, after):
    def kernel(a_ref, b_ref, after_ref, own_ref, send_ref):
        own_ref[...] = a_ref[0].astype(F32) + b_ref[0].astype(F32)
        send_ref[...] = (a_ref[1].astype(F32) + b_ref[1].astype(F32)).astype(BF16)

    block = keep.shape[1:]
    return call(
        kernel,
        [like(block, F32), like(block, BF16)],
        SLOW,
        in_specs=[VMEM] * 2 + [ANY],
        out_specs=[VMEM] * 2,
    )(keep, got, after)


def add(parts, after):
    def kernel(*refs):
        total = refs[0][...].astype(F32)
        for ref in refs[1:-2]:
            total = total + ref[...].astype(F32)
        refs[-1][...] = total

    return call(
        kernel,
        like(parts[0].shape, F32),
        SLOW,
        in_specs=[VMEM] * len(parts) + [ANY],
        out_specs=VMEM,
    )(*parts, after)


TILE = 256


def half_product(a, half, w, dtype, plus, after):
    rows, (depth, width) = a.shape[0], w.shape

    def kernel(a_ref, w_ref, *refs):
        total = jnp.dot(a_ref[...], w_ref[...], preferred_element_type=F32)
        for ref in refs[: len(plus)]:
            total = total + ref[...].astype(F32)
        refs[-1][...] = total.astype(dtype)

    column = lambda j: (0, j)
    return call(
        kernel,
        like((rows, width), dtype),
        grid=(width // TILE,),
        in_specs=[
            pl.BlockSpec((rows, depth), lambda j: (0, half)),
            pl.BlockSpec((depth, TILE), column),
        ]
        + [pl.BlockSpec((rows, TILE), column)] * len(plus)
        + [ANY],
        out_specs=pl.BlockSpec((rows, TILE), column),
    )(a, w, *plus, after)


def products(acts, w, v, after):
    rows, depth, width = acts[0].shape[0], w.shape[0], w.shape[1]
    n = len(acts)

    def kernel(*refs):
        a_refs, (w_ref, v_ref, after_ref), outs = refs[:n], refs[n : n + 3], refs[n + 3 :]
        for j in range(0, width, TILE):
            at = slice(j, j + TILE)
            for a_ref, out_ref in zip(a_refs, outs):
                total = jnp.dot(a_ref[:, :depth], w_ref[:, at], preferred_element_type=F32)
                total = total + jnp.dot(
                    a_ref[:, depth:], v_ref[:, at], preferred_element_type=F32
                )
                out_ref[:, at] = total.astype(BF16)

    return call(
        kernel,
        [like((rows, width), BF16)] * n,
        in_specs=[VMEM] * (n + 2) + [ANY],
        out_specs=[VMEM] * n,
    )(*acts, w, v, after)


def last_sum(own, parts, scale):
    rows, width = own.shape

    def kernel(own_ref, a_ref, b_ref, scale_ref, out_ref):
        total = own_ref[...] + a_ref[...].astype(F32) + b_ref[...].astype(F32)
        out_ref[...] = (total * scale_ref[...]).astype(BF16)

    return call(kernel, like((rows, width), BF16), in_specs=[VMEM] * 4, out_specs=VMEM)(
        own, *parts, scale
    )


def shards(local_fragment, anchor, momentum, next_weights, activations, norm_gain):
    replicas = lax.axis_size("rep")
    along_x = lambda v, s: move(v, "fsdp", FSDP, 0, s)
    along_y = lambda v, s: move(v, "rep", REP, 1, s)
    mine, fragment = next_weights[0], local_fragment[0]

    other = move(mine, "fsdp", FSDP, 1, 1)
    sibling = move(fragment, "rep", REP, 2, 1)

    (a2,) = gained(activations, norm_gain, [2], norm_gain)
    far_a = along_x(a2, 2)
    a1, a3 = gained(activations, norm_gain, [1, 3], a2)
    down_a, up_a = along_x(a1, 1), along_x(a3, 3)
    scale = row_scale(activations, a1)
    (a0,) = gained(activations, norm_gain, [0], scale)

    s1 = pair_sum(fragment, sibling, 1, a0)
    y1 = along_y(s1, 1)
    s3 = pair_sum(fragment, sibling, 3, s1)
    y3 = along_y(s3, 3)
    s0 = pair_sum(fragment, sibling, 0, s3)
    own = half_product(a0, 0, mine, F32, [], s0)
    s2 = pair_sum(fragment, sibling, 2, y1)
    y2 = along_y(s2, 2)
    far = half_product(far_a, 0, mine, F32, [], s2)
    send, keep = line_sum([s0, y1, y2, y3], far)
    got = lax.ppermute(send, "rep", z_pairs(lambda z: z ^ 1))

    far = half_product(far_a, 1, other, BF16, [far], send)
    far_got = along_x(far, 2)
    to_up, to_down = products([up_a, down_a], mine, other, far)
    got_down, got_up = along_x(to_up, 1), along_x(to_down, 3)
    own = half_product(a0, 1, other, F32, [own], to_up)
    total, send = halves_sum(keep, got, own)
    got = lax.ppermute(send, "rep", z_pairs(lambda z: 3 - z))
    own = add([own, far_got], send)

    total = total + got.astype(F32)
    pseudo = anchor - total / replicas
    new_momentum = 0.9 * momentum + pseudo
    new_anchor = anchor - 0.7 * (pseudo + 0.9 * new_momentum)
    result = last_sum(own, [got_up, got_down], scale)
    return (new_anchor, new_momentum, result)


def solution(mesh):
    placed = (
        P("rep", None, "fsdp", None),
        P(None, ("fsdp", "rep"), None),
        P(None, ("fsdp", "rep"), None),
        P("rep", "fsdp", None),
        P(("rep", "fsdp"), None),
        P(),
    )
    return jax.shard_map(
        shards,
        mesh=mesh,
        in_specs=placed,
        out_specs=(
            P(None, ("fsdp", "rep"), None),
            P(None, ("fsdp", "rep"), None),
            P(("rep", "fsdp"), None),
        ),
        check_vma=False,
    )
```

```python
import functools

import jax
import jax.numpy as jnp
from jax import lax
from jax.experimental import pallas as pl
from jax.experimental.pallas import tpu as pltpu
from jax.sharding import PartitionSpec as P

F32, BF16 = jnp.float32, jnp.bfloat16
EPS = 1e-05
MIB = 1 << 20
PARAMS = pltpu.CompilerParams(vmem_limit_bytes=20 * MIB)
ANY = pl.BlockSpec(memory_space=pl.ANY)
VMEM = pl.BlockSpec(memory_space=pltpu.VMEM)


def first(at, core):
    return (at + 1 - 2 * ((at + core) % 2)) % 4


def second(at, core):
    return (at + 3 + 2 * ((at + core) % 2)) % 4


def move(value, target):
    pairs = []
    for source in range(256):
        z_hi, y, core = source // 64, source // 16 % 4, source // 8 % 2
        x, z_lo = source // 2 % 4, source % 2
        z_hi, y, core, x, z_lo = target(z_hi, y, core, x, z_lo)
        pairs.append((source, (((z_hi * 4 + y) * 2 + core) * 4 + x) * 2 + z_lo))
    return lax.ppermute(value, ("rep", "fsdp"), pairs)


SLOW = 1 << 28
HBM = pl.BlockSpec(memory_space=pltpu.HBM)
DMA = pltpu.SemaphoreType.DMA


def like(shape, dtype):
    return jax.ShapeDtypeStruct(shape, dtype)


def x_of():
    return lax.axis_index("fsdp") // 2


def z_lo_of():
    return lax.axis_index("fsdp") % 2


def z_hi_of():
    return lax.axis_index("rep") // 8


def y_of():
    return lax.axis_index("rep") // 2 % 4


def core_of():
    return lax.axis_index("rep") % 2


def call(kernel, out_shape, flops=0, **rest):
    cost = pl.CostEstimate(flops=flops, bytes_accessed=0, transcendentals=0)
    return pl.pallas_call(
        kernel, out_shape=out_shape, compiler_params=PARAMS, cost_estimate=cost, **rest
    )


def in_hbm(array):
    return pltpu.with_memory_space_constraint(array, pltpu.HBM)


def gained(activations, norm_gain, owners, after):
    rows, step, n = activations.shape[0], 1024, 2 * len(owners)

    def kernel(a_ref, g_ref, after_ref, *refs):
        outs, (a_buf, sems), g_bufs = refs[: n // 2], refs[n // 2 : n // 2 + 2], refs[n // 2 + 2 :]
        copies = []
        for k in range(n):
            place = owners[k // 2]() * 2 + (z_lo_of() + k % 2) % 2
            at = pl.ds(pl.multiple_of(place * step, step), step)
            copies.append(
                (
                    pltpu.make_async_copy(g_ref.at[at], g_bufs[k], sems.at[2 * k]),
                    pltpu.make_async_copy(a_ref.at[:, at], a_buf.at[k], sems.at[2 * k + 1]),
                )
            )
            for copy in copies[-1]:
                copy.start()
        for k in range(n):
            for copy in copies[k]:
                copy.wait()
            value = a_buf[k].astype(F32) * g_bufs[k][...].reshape(1, step)
            outs[k // 2][:, k % 2 * step : (k % 2 + 1) * step] = value.astype(BF16)

    return call(
        kernel,
        [like((rows, 2 * step), BF16)] * (n // 2),
        in_specs=[HBM, HBM, ANY],
        out_specs=[VMEM] * (n // 2),
        scratch_shapes=[pltpu.VMEM((n, rows, step), BF16), DMA((2 * n,))]
        + [pltpu.VMEM((step,), F32)] * n,
    )(in_hbm(activations), in_hbm(norm_gain), after)


def row_scale(activations, after):
    rows, width = activations.shape
    tile = 64

    def kernel(a_ref, after_ref, out_ref):
        wide = a_ref[...].astype(F32)
        out_ref[...] = lax.rsqrt(jnp.mean(wide * wide, axis=-1, keepdims=True) + EPS)

    return call(
        kernel,
        like((rows, 1), F32),
        grid=(rows // tile,),
        in_specs=[pl.BlockSpec((tile, width), lambda i: (i, 0)), ANY],
        out_specs=pl.BlockSpec((tile, 1), lambda i: (i, 0)),
    )(activations, after)


def pair_sum(mine, got, owners, after):
    shape = (2, 4, 4, 2, 32, 1024)

    def kernel(a_ref, b_ref, after_ref, out_ref):
        total = a_ref[...].astype(F32) + b_ref[...].astype(F32)
        out_ref[...] = total.astype(BF16).reshape(out_ref.shape)

    def place(i):
        return owners[0]() * (1 - i) + owners[1]() * i

    block = pl.BlockSpec((2, 4, 1, 1, 32, 1024), lambda i: (0, 0, place(i), core_of(), 0, 0))
    return call(
        kernel,
        like((2, 2, 4, 32, 1024), BF16),
        grid=(2,),
        in_specs=[block, block, ANY],
        out_specs=pl.BlockSpec((1, 2, 4, 32, 1024), lambda i: (i, 0, 0, 0, 0)),
    )(mine.reshape(shape), got.reshape(shape), after)


def halves_sum(keep, got, after, flops=0):
    def kernel(a_ref, b_ref, after_ref, own_ref, send_ref):
        own_ref[...] = a_ref[0].astype(F32) + b_ref[0].astype(F32)
        send_ref[...] = (a_ref[1].astype(F32) + b_ref[1].astype(F32)).astype(BF16)

    block = keep.shape[1:]
    return call(
        kernel,
        [like(block, F32), like(block, BF16)],
        flops,
        in_specs=[VMEM] * 2 + [ANY],
        out_specs=[VMEM] * 2,
    )(keep, got, after)


def line_sum(own, got, after):
    def kernel(a_ref, b_ref, after_ref, send_ref, keep_ref):
        z_hi, core = z_hi_of(), core_of()
        owners = (first(z_hi, core), (z_hi + 2) % 4, z_hi, second(z_hi, core))
        for i, at in enumerate(owners):
            total = a_ref[:, at] + b_ref[:, at].astype(F32)
            (send_ref, keep_ref)[i // 2][i % 2] = total.astype(BF16)

    return call(
        kernel,
        [like((2, 2, 32, 1024), BF16)] * 2,
        in_specs=[VMEM] * 2 + [ANY],
        out_specs=[VMEM] * 2,
    )(own, got, after)


TILE = 256


def half_product(a, half, w, dtype, plus, after):
    rows, (depth, width) = a.shape[0], w.shape

    def kernel(a_ref, w_ref, *refs):
        total = jnp.dot(a_ref[...], w_ref[...], preferred_element_type=F32)
        for ref in refs[: len(plus)]:
            total = total + ref[...].astype(F32)
        refs[-1][...] = total.astype(dtype)

    column = lambda j: (0, j)
    return call(
        kernel,
        like((rows, width), dtype),
        grid=(width // TILE,),
        in_specs=[
            pl.BlockSpec((rows, depth), lambda j: (0, half)),
            pl.BlockSpec((depth, TILE), column),
        ]
        + [pl.BlockSpec((rows, TILE), column)] * len(plus)
        + [ANY],
        out_specs=pl.BlockSpec((rows, TILE), column),
    )(a, w, *plus, after)


def product(a, w, v, dtype, after):
    rows, depth, width = a.shape[0], w.shape[0], w.shape[1]

    def kernel(a_ref, w_ref, v_ref, after_ref, out_ref):
        for j in range(0, width, TILE):
            at = slice(j, j + TILE)
            total = jnp.dot(a_ref[:, :depth], w_ref[:, at], preferred_element_type=F32)
            total = total + jnp.dot(a_ref[:, depth:], v_ref[:, at], preferred_element_type=F32)
            out_ref[:, at] = total.astype(dtype)

    return call(
        kernel, like((rows, width), dtype), in_specs=[VMEM] * 3 + [ANY], out_specs=VMEM
    )(a, w, v, after)


def far_product(a, w, plus, after):
    rows, (depth, width) = a.shape[0], w.shape

    def kernel(a_ref, w_ref, plus_ref, after_ref, out_ref):
        for j in range(0, width, TILE):
            at = slice(j, j + TILE)
            total = jnp.dot(a_ref[:, depth:], w_ref[:, at], preferred_element_type=F32)
            out_ref[:, at] = (total + plus_ref[:, at]).astype(BF16)

    return call(
        kernel, like((rows, width), BF16), in_specs=[VMEM] * 3 + [ANY], out_specs=VMEM
    )(a, w, plus, after)


def plus(own, got, dtype, after, flops=0):
    def kernel(own_ref, got_ref, after_ref, out_ref):
        out_ref[...] = (own_ref[...] + got_ref[...].astype(F32)).astype(dtype)

    return call(
        kernel, like(own.shape, dtype), flops, in_specs=[VMEM] * 2 + [ANY], out_specs=VMEM
    )(own, got, after)


def last_sum(own, got, scale):
    def kernel(own_ref, got_ref, scale_ref, out_ref):
        out_ref[...] = ((own_ref[...] + got_ref[...].astype(F32)) * scale_ref[...]).astype(BF16)

    return call(kernel, like(own.shape, BF16), in_specs=[VMEM] * 3, out_specs=VMEM)(
        own, got, scale
    )


def shards(local_fragment, anchor, momentum, next_weights, activations, norm_gain):
    replicas = lax.axis_size("rep")
    mine, fragment = next_weights[0], local_fragment[0]
    x_first = lambda v: move(v, lambda z, y, c, x, l: (z, y, c, first(x, c), l))
    x_second = lambda v: move(v, lambda z, y, c, x, l: (z, y, c, second(x, c), l))
    x_far = lambda v: move(v, lambda z, y, c, x, l: (z, y, c, (x + 2) % 4, l))
    y_first = lambda v: move(v, lambda z, y, c, x, l: (z, first(y, c), c, x, l))
    y_second = lambda v: move(v, lambda z, y, c, x, l: (z, second(y, c), c, x, l))
    z_first = lambda v: move(v, lambda z, y, c, x, l: (first(z, c), y, c, x, l))
    z_second = lambda v: move(v, lambda z, y, c, x, l: (second(z, c), y, c, x, l))

    other = move(mine, lambda z, y, c, x, l: (z, y, c, x, 1 - l))
    sibling = move(fragment, lambda z, y, c, x, l: (z, y, 1 - c, x, l))

    (a_far,) = gained(activations, norm_gain, [lambda: (x_of() + 2) % 4], norm_gain)
    far_a = x_far(a_far)
    a_first, a_second = gained(
        activations,
        norm_gain,
        [lambda: first(x_of(), core_of()), lambda: second(x_of(), core_of())],
        a_far,
    )
    first_a, second_a = x_first(a_first), x_second(a_second)
    scale = row_scale(activations, a_first)
    (own_a,) = gained(activations, norm_gain, [x_of], scale)

    send = pair_sum(
        fragment, sibling, [lambda: first(y_of(), core_of()), lambda: (y_of() + 2) % 4], own_a
    )
    got = y_first(send)
    keep = pair_sum(fragment, sibling, [y_of, lambda: second(y_of(), core_of())], send)
    own = half_product(own_a, 0, mine, F32, [], keep)
    far = half_product(far_a, 0, mine, F32, [], own)
    line, send = halves_sum(keep, got, far)
    got = y_second(send)

    far = far_product(far_a, other, far, send)
    via = x_first(far)
    send, keep = line_sum(line, got, far)
    got = z_first(send)
    near = product(first_a, mine, other, BF16, send)
    from_first = x_first(near)
    part = product(second_a, mine, other, F32, near)
    own = half_product(own_a, 1, other, F32, [own], part)
    from_second = x_second(plus(part, via, BF16, own))
    total, send = halves_sum(keep, got, part, SLOW)
    got = z_second(send)
    own = plus(own, from_first, F32, send, SLOW)

    total = total + got.astype(F32)
    pseudo = anchor - total / replicas
    new_momentum = 0.9 * momentum + pseudo
    new_anchor = anchor - 0.7 * (pseudo + 0.9 * new_momentum)
    result = last_sum(own, from_second, scale)
    return (new_anchor, new_momentum, result)


def solution(mesh):
    placed = (
        P("rep", None, "fsdp", None),
        P(None, ("fsdp", "rep"), None),
        P(None, ("fsdp", "rep"), None),
        P("rep", "fsdp", None),
        P(("rep", "fsdp"), None),
        P(),
    )
    return jax.shard_map(
        shards,
        mesh=mesh,
        in_specs=placed,
        out_specs=(
            P(None, ("fsdp", "rep"), None),
            P(None, ("fsdp", "rep"), None),
            P(("rep", "fsdp"), None),
        ),
        check_vma=False,
    )
```

```python
import functools

import jax
import jax.numpy as jnp
from jax import lax
from jax.experimental import pallas as pl
from jax.experimental.pallas import tpu as pltpu
from jax.sharding import PartitionSpec as P

F32, BF16 = jnp.float32, jnp.bfloat16
EPS = 1e-05
MIB = 1 << 20
PARAMS = pltpu.CompilerParams(vmem_limit_bytes=20 * MIB)
ANY = pl.BlockSpec(memory_space=pl.ANY)
VMEM = pl.BlockSpec(memory_space=pltpu.VMEM)


def first(at, core):
    return (at + 1 - 2 * ((at + core) % 2)) % 4


def second(at, core):
    return (at + 3 + 2 * ((at + core) % 2)) % 4


def move(value, target):
    pairs = []
    for source in range(256):
        z_hi, y, core = source // 64, source // 16 % 4, source // 8 % 2
        x, z_lo = source // 2 % 4, source % 2
        z_hi, y, core, x, z_lo = target(z_hi, y, core, x, z_lo)
        pairs.append((source, (((z_hi * 4 + y) * 2 + core) * 4 + x) * 2 + z_lo))
    return lax.ppermute(value, ("rep", "fsdp"), pairs)


SLOW = 1 << 28
HBM = pl.BlockSpec(memory_space=pltpu.HBM)
DMA = pltpu.SemaphoreType.DMA


def like(shape, dtype):
    return jax.ShapeDtypeStruct(shape, dtype)


def x_of():
    return lax.axis_index("fsdp") // 2


def z_lo_of():
    return lax.axis_index("fsdp") % 2


def z_hi_of():
    return lax.axis_index("rep") // 8


def y_of():
    return lax.axis_index("rep") // 2 % 4


def core_of():
    return lax.axis_index("rep") % 2


def call(kernel, out_shape, flops=0, **rest):
    cost = pl.CostEstimate(flops=flops, bytes_accessed=0, transcendentals=0)
    return pl.pallas_call(
        kernel, out_shape=out_shape, compiler_params=PARAMS, cost_estimate=cost, **rest
    )


def in_hbm(array):
    return pltpu.with_memory_space_constraint(array, pltpu.HBM)


def gained(activations, norm_gain, owners, after):
    rows, step, n = activations.shape[0], 1024, 2 * len(owners)

    cuts = 4
    tile = rows // cuts

    def kernel(a_ref, g_ref, after_ref, *refs):
        outs, (a_buf, a_sems, g_sems) = refs[: n // 2], refs[n // 2 : n // 2 + 3]
        g_bufs = refs[n // 2 + 3 :]
        a_copies, g_copies = [], []
        for k in range(n):
            place = owners[k // 2]() * 2 + (z_lo_of() + k % 2) % 2
            at = pl.ds(pl.multiple_of(place * step, step), step)
            g_copies.append(pltpu.make_async_copy(g_ref.at[at], g_bufs[k], g_sems.at[k]))
            g_copies[-1].start()
            for i in range(cuts):
                part = slice(i * tile, (i + 1) * tile)
                a_copies.append(
                    pltpu.make_async_copy(
                        a_ref.at[part, at], a_buf.at[k, part], a_sems.at[k * cuts + i]
                    )
                )
                a_copies[-1].start()
        for k in range(n):
            g_copies[k].wait()
            gain = g_bufs[k][...].reshape(1, step)
            for i in range(cuts):
                part = slice(i * tile, (i + 1) * tile)
                a_copies[k * cuts + i].wait()
                value = a_buf[k, part].astype(F32) * gain
                outs[k // 2][part, k % 2 * step : (k % 2 + 1) * step] = value.astype(BF16)

    return call(
        kernel,
        [like((rows, 2 * step), BF16)] * (n // 2),
        in_specs=[HBM, HBM, ANY],
        out_specs=[VMEM] * (n // 2),
        scratch_shapes=[pltpu.VMEM((n, rows, step), BF16), DMA((cuts * n,)), DMA((n,))]
        + [pltpu.VMEM((step,), F32)] * n,
    )(in_hbm(activations), in_hbm(norm_gain), after)


def row_scale(activations, after):
    rows, width = activations.shape
    tile = 64

    def kernel(a_ref, after_ref, out_ref):
        wide = a_ref[...].astype(F32)
        out_ref[...] = lax.rsqrt(jnp.mean(wide * wide, axis=-1, keepdims=True) + EPS)

    return call(
        kernel,
        like((rows, 1), F32),
        grid=(rows // tile,),
        in_specs=[pl.BlockSpec((tile, width), lambda i: (i, 0)), ANY],
        out_specs=pl.BlockSpec((tile, 1), lambda i: (i, 0)),
    )(activations, after)


def pair_sum(mine, got, owners, after):
    shape = (2, 4, 4, 2, 32, 1024)

    def kernel(a_ref, b_ref, after_ref, out_ref):
        total = a_ref[...].astype(F32) + b_ref[...].astype(F32)
        out_ref[...] = total.astype(BF16).reshape(out_ref.shape)

    def place(i):
        return owners[0]() * (1 - i) + owners[1]() * i

    block = pl.BlockSpec((2, 4, 1, 1, 32, 1024), lambda i: (0, 0, place(i), core_of(), 0, 0))
    return call(
        kernel,
        like((2, 2, 4, 32, 1024), BF16),
        grid=(2,),
        in_specs=[block, block, ANY],
        out_specs=pl.BlockSpec((1, 2, 4, 32, 1024), lambda i: (i, 0, 0, 0, 0)),
    )(mine.reshape(shape), got.reshape(shape), after)


def halves_sum(keep, got, after, flops=0):
    def kernel(a_ref, b_ref, after_ref, own_ref, send_ref):
        own_ref[...] = a_ref[0].astype(F32) + b_ref[0].astype(F32)
        send_ref[...] = (a_ref[1].astype(F32) + b_ref[1].astype(F32)).astype(BF16)

    block = keep.shape[1:]
    return call(
        kernel,
        [like(block, F32), like(block, BF16)],
        flops,
        in_specs=[VMEM] * 2 + [ANY],
        out_specs=[VMEM] * 2,
    )(keep, got, after)


def line_sum(own, got, after):
    def kernel(a_ref, b_ref, after_ref, send_ref, keep_ref):
        z_hi, core = z_hi_of(), core_of()
        owners = (first(z_hi, core), (z_hi + 2) % 4, z_hi, second(z_hi, core))
        for i, at in enumerate(owners):
            total = a_ref[:, at] + b_ref[:, at].astype(F32)
            (send_ref, keep_ref)[i // 2][i % 2] = total.astype(BF16)

    return call(
        kernel,
        [like((2, 2, 32, 1024), BF16)] * 2,
        in_specs=[VMEM] * 2 + [ANY],
        out_specs=[VMEM] * 2,
    )(own, got, after)


TILE = 256


def half_product(a, half, w, dtype, plus, after):
    rows, (depth, width) = a.shape[0], w.shape

    def kernel(a_ref, w_ref, *refs):
        total = jnp.dot(a_ref[...], w_ref[...], preferred_element_type=F32)
        for ref in refs[: len(plus)]:
            total = total + ref[...].astype(F32)
        refs[-1][...] = total.astype(dtype)

    column = lambda j: (0, j)
    return call(
        kernel,
        like((rows, width), dtype),
        grid=(width // TILE,),
        in_specs=[
            pl.BlockSpec((rows, depth), lambda j: (0, half)),
            pl.BlockSpec((depth, TILE), column),
        ]
        + [pl.BlockSpec((rows, TILE), column)] * len(plus)
        + [ANY],
        out_specs=pl.BlockSpec((rows, TILE), column),
    )(a, w, *plus, after)


def product(a, w, v, dtype, after):
    rows, depth, width = a.shape[0], w.shape[0], w.shape[1]

    def kernel(a_ref, w_ref, v_ref, after_ref, out_ref):
        for j in range(0, width, TILE):
            at = slice(j, j + TILE)
            total = jnp.dot(a_ref[:, :depth], w_ref[:, at], preferred_element_type=F32)
            total = total + jnp.dot(a_ref[:, depth:], v_ref[:, at], preferred_element_type=F32)
            out_ref[:, at] = total.astype(dtype)

    return call(
        kernel, like((rows, width), dtype), in_specs=[VMEM] * 3 + [ANY], out_specs=VMEM
    )(a, w, v, after)


def far_product(a, w, plus, after):
    rows, (depth, width) = a.shape[0], w.shape

    def kernel(a_ref, w_ref, plus_ref, after_ref, out_ref):
        for j in range(0, width, TILE):
            at = slice(j, j + TILE)
            total = jnp.dot(a_ref[:, depth:], w_ref[:, at], preferred_element_type=F32)
            out_ref[:, at] = (total + plus_ref[:, at]).astype(BF16)

    return call(
        kernel, like((rows, width), BF16), in_specs=[VMEM] * 3 + [ANY], out_specs=VMEM
    )(a, w, plus, after)


def plus(own, got, dtype, after, flops=0):
    def kernel(own_ref, got_ref, after_ref, out_ref):
        out_ref[...] = (own_ref[...] + got_ref[...].astype(F32)).astype(dtype)

    return call(
        kernel, like(own.shape, dtype), flops, in_specs=[VMEM] * 2 + [ANY], out_specs=VMEM
    )(own, got, after)


def last_sum(own, got, scale):
    rows, width = own.shape
    cuts = 4
    tile = rows // cuts

    def kernel(own_ref, got_ref, scale_ref, out_ref, buf, sems):
        copies = []
        for i in range(cuts):
            part = slice(i * tile, (i + 1) * tile)
            total = own_ref[part] + got_ref[part].astype(F32)
            buf[part] = (total * scale_ref[part]).astype(BF16)
            copies.append(pltpu.make_async_copy(buf.at[part], out_ref.at[part], sems.at[i]))
            copies[-1].start()
        for copy in copies:
            copy.wait()

    return call(
        kernel,
        like(own.shape, BF16),
        in_specs=[VMEM] * 3,
        out_specs=ANY,
        scratch_shapes=[pltpu.VMEM((rows, width), BF16), DMA((cuts,))],
    )(own, got, scale)


def shards(local_fragment, anchor, momentum, next_weights, activations, norm_gain):
    replicas = lax.axis_size("rep")
    mine, fragment = next_weights[0], local_fragment[0]
    x_first = lambda v: move(v, lambda z, y, c, x, l: (z, y, c, first(x, c), l))
    x_second = lambda v: move(v, lambda z, y, c, x, l: (z, y, c, second(x, c), l))
    x_far = lambda v: move(v, lambda z, y, c, x, l: (z, y, c, (x + 2) % 4, l))
    y_first = lambda v: move(v, lambda z, y, c, x, l: (z, first(y, c), c, x, l))
    y_second = lambda v: move(v, lambda z, y, c, x, l: (z, second(y, c), c, x, l))
    z_first = lambda v: move(v, lambda z, y, c, x, l: (first(z, c), y, c, x, l))
    z_second = lambda v: move(v, lambda z, y, c, x, l: (second(z, c), y, c, x, l))

    other = move(mine, lambda z, y, c, x, l: (z, y, c, x, 1 - l))
    sibling = move(fragment, lambda z, y, c, x, l: (z, y, 1 - c, x, l))

    (a_far,) = gained(activations, norm_gain, [lambda: (x_of() + 2) % 4], norm_gain)
    far_a = x_far(a_far)
    a_first, a_second = gained(
        activations,
        norm_gain,
        [lambda: first(x_of(), core_of()), lambda: second(x_of(), core_of())],
        a_far,
    )
    first_a, second_a = x_first(a_first), x_second(a_second)
    scale = row_scale(activations, a_first)
    (own_a,) = gained(activations, norm_gain, [x_of], scale)

    send = pair_sum(
        fragment, sibling, [lambda: first(y_of(), core_of()), lambda: (y_of() + 2) % 4], own_a
    )
    got = y_first(send)
    keep = pair_sum(fragment, sibling, [y_of, lambda: second(y_of(), core_of())], send)
    own = half_product(own_a, 0, mine, F32, [], keep)
    far = half_product(far_a, 0, mine, F32, [], own)
    line, send = halves_sum(keep, got, far)
    got = y_second(send)

    far = far_product(far_a, other, far, send)
    via = x_first(far)
    send, keep = line_sum(line, got, far)
    got = z_first(send)
    near = product(first_a, mine, other, BF16, send)
    from_first = x_first(near)
    part = product(second_a, mine, other, F32, near)
    from_second = x_second(plus(part, via, BF16, part))
    total, send = halves_sum(keep, got, part, SLOW)
    got = z_second(send)
    own = half_product(own_a, 1, other, F32, [own], send)
    own = plus(own, from_first, F32, own, SLOW)

    total = total + got.astype(F32)
    pseudo = anchor - total / replicas
    new_momentum = 0.9 * momentum + pseudo
    new_anchor = anchor - 0.7 * (pseudo + 0.9 * new_momentum)
    result = last_sum(own, from_second, scale)
    return (new_anchor, new_momentum, result)


def solution(mesh):
    placed = (
        P("rep", None, "fsdp", None),
        P(None, ("fsdp", "rep"), None),
        P(None, ("fsdp", "rep"), None),
        P("rep", "fsdp", None),
        P(("rep", "fsdp"), None),
        P(),
    )
    return jax.shard_map(
        shards,
        mesh=mesh,
        in_specs=placed,
        out_specs=(
            P(None, ("fsdp", "rep"), None),
            P(None, ("fsdp", "rep"), None),
            P(("rep", "fsdp"), None),
        ),
        check_vma=False,
    )
```

```python
import functools

import jax
import jax.numpy as jnp
from jax import lax
from jax.experimental import pallas as pl
from jax.experimental.pallas import tpu as pltpu
from jax.sharding import PartitionSpec as P

F32, BF16 = jnp.float32, jnp.bfloat16
EPS = 1e-05
MIB = 1 << 20
PARAMS = pltpu.CompilerParams(vmem_limit_bytes=20 * MIB)
ANY = pl.BlockSpec(memory_space=pl.ANY)
VMEM = pl.BlockSpec(memory_space=pltpu.VMEM)


def first(at, core):
    return (at + 1 - 2 * ((at + core) % 2)) % 4


def second(at, core):
    return (at + 3 + 2 * ((at + core) % 2)) % 4


def move(value, target):
    pairs = []
    for source in range(256):
        z_hi, y, core = source // 64, source // 16 % 4, source // 8 % 2
        x, z_lo = source // 2 % 4, source % 2
        z_hi, y, core, x, z_lo = target(z_hi, y, core, x, z_lo)
        pairs.append((source, (((z_hi * 4 + y) * 2 + core) * 4 + x) * 2 + z_lo))
    return lax.ppermute(value, ("rep", "fsdp"), pairs)


SLOW = 1 << 28
HBM = pl.BlockSpec(memory_space=pltpu.HBM)
DMA = pltpu.SemaphoreType.DMA


def like(shape, dtype):
    return jax.ShapeDtypeStruct(shape, dtype)


def x_of():
    return lax.axis_index("fsdp") // 2


def z_lo_of():
    return lax.axis_index("fsdp") % 2


def z_hi_of():
    return lax.axis_index("rep") // 8


def y_of():
    return lax.axis_index("rep") // 2 % 4


def core_of():
    return lax.axis_index("rep") % 2


def call(kernel, out_shape, flops=0, **rest):
    cost = pl.CostEstimate(flops=flops, bytes_accessed=0, transcendentals=0)
    return pl.pallas_call(
        kernel, out_shape=out_shape, compiler_params=PARAMS, cost_estimate=cost, **rest
    )


def in_hbm(array):
    return pltpu.with_memory_space_constraint(array, pltpu.HBM)


def gained(activations, norm_gain, owners, after):
    rows, step, n = activations.shape[0], 1024, 2 * len(owners)

    cuts = 4
    tile = rows // cuts

    def kernel(a_ref, g_ref, after_ref, *refs):
        outs, (a_buf, a_sems, g_sems) = refs[: n // 2], refs[n // 2 : n // 2 + 3]
        g_bufs = refs[n // 2 + 3 :]
        a_copies, g_copies = [], []
        for k in range(n):
            place = owners[k // 2]() * 2 + (z_lo_of() + k % 2) % 2
            at = pl.ds(pl.multiple_of(place * step, step), step)
            g_copies.append(pltpu.make_async_copy(g_ref.at[at], g_bufs[k], g_sems.at[k]))
            g_copies[-1].start()
            for i in range(cuts):
                part = slice(i * tile, (i + 1) * tile)
                a_copies.append(
                    pltpu.make_async_copy(
                        a_ref.at[part, at], a_buf.at[k, part], a_sems.at[k * cuts + i]
                    )
                )
                a_copies[-1].start()
        for k in range(n):
            g_copies[k].wait()
            gain = g_bufs[k][...].reshape(1, step)
            for i in range(cuts):
                part = slice(i * tile, (i + 1) * tile)
                a_copies[k * cuts + i].wait()
                value = a_buf[k, part].astype(F32) * gain
                outs[k // 2][part, k % 2 * step : (k % 2 + 1) * step] = value.astype(BF16)

    return call(
        kernel,
        [like((rows, 2 * step), BF16)] * (n // 2),
        in_specs=[HBM, HBM, ANY],
        out_specs=[VMEM] * (n // 2),
        scratch_shapes=[pltpu.VMEM((n, rows, step), BF16), DMA((cuts * n,)), DMA((n,))]
        + [pltpu.VMEM((step,), F32)] * n,
    )(in_hbm(activations), in_hbm(norm_gain), after)


def row_scale(activations, after):
    rows, width = activations.shape
    tile = 64

    def kernel(a_ref, after_ref, out_ref):
        wide = a_ref[...].astype(F32)
        out_ref[...] = lax.rsqrt(jnp.mean(wide * wide, axis=-1, keepdims=True) + EPS)

    return call(
        kernel,
        like((rows, 1), F32),
        grid=(rows // tile,),
        in_specs=[pl.BlockSpec((tile, width), lambda i: (i, 0)), ANY],
        out_specs=pl.BlockSpec((tile, 1), lambda i: (i, 0)),
    )(activations, after)


def pair_sum(mine, got, owners, after):
    shape = (2, 4, 4, 2, 32, 1024)

    def kernel(a_ref, b_ref, after_ref, out_ref):
        total = a_ref[...].astype(F32) + b_ref[...].astype(F32)
        out_ref[...] = total.astype(BF16).reshape(out_ref.shape)

    def place(i):
        return owners[0]() * (1 - i) + owners[1]() * i

    block = pl.BlockSpec((2, 4, 1, 1, 32, 1024), lambda i: (0, 0, place(i), core_of(), 0, 0))
    return call(
        kernel,
        like((2, 2, 4, 32, 1024), BF16),
        grid=(2,),
        in_specs=[block, block, ANY],
        out_specs=pl.BlockSpec((1, 2, 4, 32, 1024), lambda i: (i, 0, 0, 0, 0)),
    )(mine.reshape(shape), got.reshape(shape), after)


def halves_sum(keep, got, after, flops=0):
    def kernel(a_ref, b_ref, after_ref, own_ref, send_ref):
        own_ref[...] = a_ref[0].astype(F32) + b_ref[0].astype(F32)
        send_ref[...] = (a_ref[1].astype(F32) + b_ref[1].astype(F32)).astype(BF16)

    block = keep.shape[1:]
    return call(
        kernel,
        [like(block, F32), like(block, BF16)],
        flops,
        in_specs=[VMEM] * 2 + [ANY],
        out_specs=[VMEM] * 2,
    )(keep, got, after)


def line_sum(own, got, after):
    def kernel(a_ref, b_ref, after_ref, send_ref, keep_ref):
        z_hi, core = z_hi_of(), core_of()
        owners = (first(z_hi, core), (z_hi + 2) % 4, z_hi, second(z_hi, core))
        for i, at in enumerate(owners):
            total = a_ref[:, at] + b_ref[:, at].astype(F32)
            (send_ref, keep_ref)[i // 2][i % 2] = total.astype(BF16)

    return call(
        kernel,
        [like((2, 2, 32, 1024), BF16)] * 2,
        in_specs=[VMEM] * 2 + [ANY],
        out_specs=[VMEM] * 2,
    )(own, got, after)


TILE = 512


def half_product(a, half, w, dtype, plus, after):
    rows, (depth, width) = a.shape[0], w.shape

    def kernel(a_ref, w_ref, *refs):
        total = jnp.dot(a_ref[...], w_ref[...], preferred_element_type=F32)
        for ref in refs[: len(plus)]:
            total = total + ref[...].astype(F32)
        refs[-1][...] = total.astype(dtype)

    column = lambda j: (0, j)
    return call(
        kernel,
        like((rows, width), dtype),
        grid=(width // TILE,),
        in_specs=[
            pl.BlockSpec((rows, depth), lambda j: (0, half)),
            pl.BlockSpec((depth, TILE), column),
        ]
        + [pl.BlockSpec((rows, TILE), column)] * len(plus)
        + [ANY],
        out_specs=pl.BlockSpec((rows, TILE), column),
    )(a, w, *plus, after)


def product(a, w, v, dtype, after):
    rows, depth, width = a.shape[0], w.shape[0], w.shape[1]

    def kernel(a_ref, w_ref, v_ref, after_ref, out_ref):
        for j in range(0, width, TILE):
            at = slice(j, j + TILE)
            total = jnp.dot(a_ref[:, :depth], w_ref[:, at], preferred_element_type=F32)
            total = total + jnp.dot(a_ref[:, depth:], v_ref[:, at], preferred_element_type=F32)
            out_ref[:, at] = total.astype(dtype)

    return call(
        kernel, like((rows, width), dtype), in_specs=[VMEM] * 3 + [ANY], out_specs=VMEM
    )(a, w, v, after)


def far_product(a, w, plus, after):
    rows, (depth, width) = a.shape[0], w.shape

    def kernel(a_ref, w_ref, plus_ref, after_ref, out_ref):
        for j in range(0, width, TILE):
            at = slice(j, j + TILE)
            total = jnp.dot(a_ref[:, depth:], w_ref[:, at], preferred_element_type=F32)
            out_ref[:, at] = (total + plus_ref[:, at]).astype(BF16)

    return call(
        kernel, like((rows, width), BF16), in_specs=[VMEM] * 3 + [ANY], out_specs=VMEM
    )(a, w, plus, after)


def plus(own, got, dtype, after, flops=0):
    def kernel(own_ref, got_ref, after_ref, out_ref):
        out_ref[...] = (own_ref[...] + got_ref[...].astype(F32)).astype(dtype)

    return call(
        kernel, like(own.shape, dtype), flops, in_specs=[VMEM] * 2 + [ANY], out_specs=VMEM
    )(own, got, after)


def last_sum(own, got, scale):
    rows, width = own.shape
    cuts = 4
    tile = rows // cuts

    def kernel(own_ref, got_ref, scale_ref, out_ref, buf, sems):
        copies = []
        for i in range(cuts):
            part = slice(i * tile, (i + 1) * tile)
            total = own_ref[part] + got_ref[part].astype(F32)
            buf[part] = (total * scale_ref[part]).astype(BF16)
            copies.append(pltpu.make_async_copy(buf.at[part], out_ref.at[part], sems.at[i]))
            copies[-1].start()
        for copy in copies:
            copy.wait()

    return call(
        kernel,
        like(own.shape, BF16),
        in_specs=[VMEM] * 3,
        out_specs=ANY,
        scratch_shapes=[pltpu.VMEM((rows, width), BF16), DMA((cuts,))],
    )(own, got, scale)


def shards(local_fragment, anchor, momentum, next_weights, activations, norm_gain):
    replicas = lax.axis_size("rep")
    mine, fragment = next_weights[0], local_fragment[0]
    x_first = lambda v: move(v, lambda z, y, c, x, l: (z, y, c, first(x, c), l))
    x_second = lambda v: move(v, lambda z, y, c, x, l: (z, y, c, second(x, c), l))
    x_far = lambda v: move(v, lambda z, y, c, x, l: (z, y, c, (x + 2) % 4, l))
    y_first = lambda v: move(v, lambda z, y, c, x, l: (z, first(y, c), c, x, l))
    y_second = lambda v: move(v, lambda z, y, c, x, l: (z, second(y, c), c, x, l))
    z_first = lambda v: move(v, lambda z, y, c, x, l: (first(z, c), y, c, x, l))
    z_second = lambda v: move(v, lambda z, y, c, x, l: (second(z, c), y, c, x, l))

    other = move(mine, lambda z, y, c, x, l: (z, y, c, x, 1 - l))
    sibling = move(fragment, lambda z, y, c, x, l: (z, y, 1 - c, x, l))

    (a_far,) = gained(activations, norm_gain, [lambda: (x_of() + 2) % 4], norm_gain)
    far_a = x_far(a_far)
    a_first, a_second = gained(
        activations,
        norm_gain,
        [lambda: first(x_of(), core_of()), lambda: second(x_of(), core_of())],
        a_far,
    )
    first_a, second_a = x_first(a_first), x_second(a_second)
    scale = row_scale(activations, a_first)
    (own_a,) = gained(activations, norm_gain, [x_of], scale)

    send = pair_sum(
        fragment, sibling, [lambda: first(y_of(), core_of()), lambda: (y_of() + 2) % 4], own_a
    )
    got = y_first(send)
    keep = pair_sum(fragment, sibling, [y_of, lambda: second(y_of(), core_of())], send)
    own = half_product(own_a, 0, mine, F32, [], keep)
    far = half_product(far_a, 0, mine, F32, [], own)
    line, send = halves_sum(keep, got, far)
    got = y_second(send)

    far = far_product(far_a, other, far, send)
    via = x_first(far)
    send, keep = line_sum(line, got, far)
    got = z_first(send)
    near = product(first_a, mine, other, BF16, send)
    from_first = x_first(near)
    part = product(second_a, mine, other, F32, near)
    from_second = x_second(plus(part, via, BF16, part))
    total, send = halves_sum(keep, got, part, SLOW)
    got = z_second(send)
    own = half_product(own_a, 1, other, F32, [own], send)
    own = plus(own, from_first, F32, own, SLOW)

    total = total + got.astype(F32)
    pseudo = anchor - total / replicas
    new_momentum = 0.9 * momentum + pseudo
    new_anchor = anchor - 0.7 * (pseudo + 0.9 * new_momentum)
    result = last_sum(own, from_second, scale)
    return (new_anchor, new_momentum, result)


def solution(mesh):
    placed = (
        P("rep", None, "fsdp", None),
        P(None, ("fsdp", "rep"), None),
        P(None, ("fsdp", "rep"), None),
        P("rep", "fsdp", None),
        P(("rep", "fsdp"), None),
        P(),
    )
    return jax.shard_map(
        shards,
        mesh=mesh,
        in_specs=placed,
        out_specs=(
            P(None, ("fsdp", "rep"), None),
            P(None, ("fsdp", "rep"), None),
            P(("rep", "fsdp"), None),
        ),
        check_vma=False,
    )
```

```python
import functools

import jax
import jax.numpy as jnp
from jax import lax
from jax.experimental import pallas as pl
from jax.experimental.pallas import tpu as pltpu
from jax.sharding import PartitionSpec as P

F32, BF16 = jnp.float32, jnp.bfloat16
EPS = 1e-05
MIB = 1 << 20
PARAMS = pltpu.CompilerParams(vmem_limit_bytes=20 * MIB)
ANY = pl.BlockSpec(memory_space=pl.ANY)
VMEM = pl.BlockSpec(memory_space=pltpu.VMEM)


def first(at, core):
    return (at + 1 - 2 * ((at + core) % 2)) % 4


def second(at, core):
    return (at + 3 + 2 * ((at + core) % 2)) % 4


def move(value, target):
    pairs = []
    for source in range(256):
        z_hi, y, core = source // 64, source // 16 % 4, source // 8 % 2
        x, z_lo = source // 2 % 4, source % 2
        z_hi, y, core, x, z_lo = target(z_hi, y, core, x, z_lo)
        pairs.append((source, (((z_hi * 4 + y) * 2 + core) * 4 + x) * 2 + z_lo))
    return lax.ppermute(value, ("rep", "fsdp"), pairs)


SLOW = 1 << 28
HBM = pl.BlockSpec(memory_space=pltpu.HBM)
DMA = pltpu.SemaphoreType.DMA


def like(shape, dtype):
    return jax.ShapeDtypeStruct(shape, dtype)


def x_of():
    return lax.axis_index("fsdp") // 2


def z_lo_of():
    return lax.axis_index("fsdp") % 2


def z_hi_of():
    return lax.axis_index("rep") // 8


def y_of():
    return lax.axis_index("rep") // 2 % 4


def core_of():
    return lax.axis_index("rep") % 2


def call(kernel, out_shape, flops=0, **rest):
    cost = pl.CostEstimate(flops=flops, bytes_accessed=0, transcendentals=0)
    return pl.pallas_call(
        kernel, out_shape=out_shape, compiler_params=PARAMS, cost_estimate=cost, **rest
    )


def in_hbm(array):
    return pltpu.with_memory_space_constraint(array, pltpu.HBM)


def gained(activations, norm_gain, owners, after):
    rows, step, n = activations.shape[0], 1024, 2 * len(owners)

    cuts = 4
    tile = rows // cuts

    def kernel(a_ref, g_ref, after_ref, *refs):
        outs, (a_buf, a_sems, g_sems) = refs[: n // 2], refs[n // 2 : n // 2 + 3]
        g_bufs = refs[n // 2 + 3 :]
        a_copies, g_copies = [], []
        for k in range(n):
            place = owners[k // 2]() * 2 + (z_lo_of() + k % 2) % 2
            at = pl.ds(pl.multiple_of(place * step, step), step)
            g_copies.append(pltpu.make_async_copy(g_ref.at[at], g_bufs[k], g_sems.at[k]))
            g_copies[-1].start()
            for i in range(cuts):
                part = slice(i * tile, (i + 1) * tile)
                a_copies.append(
                    pltpu.make_async_copy(
                        a_ref.at[part, at], a_buf.at[k, part], a_sems.at[k * cuts + i]
                    )
                )
                a_copies[-1].start()
        for k in range(n):
            g_copies[k].wait()
            gain = g_bufs[k][...].reshape(1, step)
            for i in range(cuts):
                part = slice(i * tile, (i + 1) * tile)
                a_copies[k * cuts + i].wait()
                value = a_buf[k, part].astype(F32) * gain
                outs[k // 2][part, k % 2 * step : (k % 2 + 1) * step] = value.astype(BF16)

    return call(
        kernel,
        [like((rows, 2 * step), BF16)] * (n // 2),
        in_specs=[HBM, HBM, ANY],
        out_specs=[VMEM] * (n // 2),
        scratch_shapes=[pltpu.VMEM((n, rows, step), BF16), DMA((cuts * n,)), DMA((n,))]
        + [pltpu.VMEM((step,), F32)] * n,
    )(in_hbm(activations), in_hbm(norm_gain), after)


def gained_block(activations, norm_gain, owner, after):
    rows, step, cuts = activations.shape[0], 2048, 4
    tile = rows // cuts

    def kernel(a_ref, g_ref, after_ref, out_ref, a_buf, g_buf, sems):
        at = pl.ds(pl.multiple_of(owner() * step, step), step)
        copies = [pltpu.make_async_copy(g_ref.at[at], g_buf, sems.at[cuts])]
        for i in range(cuts):
            part = slice(i * tile, (i + 1) * tile)
            copies.append(
                pltpu.make_async_copy(a_ref.at[part, at], a_buf.at[part], sems.at[i])
            )
        for copy in copies:
            copy.start()
        copies[0].wait()
        gain = g_buf[...].reshape(1, step)
        for i in range(cuts):
            part = slice(i * tile, (i + 1) * tile)
            copies[1 + i].wait()
            out_ref[part] = (a_buf[part].astype(F32) * gain).astype(BF16)

    return call(
        kernel,
        like((rows, step), BF16),
        in_specs=[HBM, HBM, ANY],
        out_specs=VMEM,
        scratch_shapes=[
            pltpu.VMEM((rows, step), BF16),
            pltpu.VMEM((step,), F32),
            DMA((cuts + 1,)),
        ],
    )(in_hbm(activations), in_hbm(norm_gain), after)


def row_scale(activations, after):
    rows, width = activations.shape
    tile = 64

    def kernel(a_ref, after_ref, out_ref):
        wide = a_ref[...].astype(F32)
        out_ref[...] = lax.rsqrt(jnp.mean(wide * wide, axis=-1, keepdims=True) + EPS)

    return call(
        kernel,
        like((rows, 1), F32),
        grid=(rows // tile,),
        in_specs=[pl.BlockSpec((tile, width), lambda i: (i, 0)), ANY],
        out_specs=pl.BlockSpec((tile, 1), lambda i: (i, 0)),
    )(activations, after)


def pair_sum(mine, got, owners, after):
    shape = (2, 4, 4, 2, 32, 1024)

    def kernel(a_ref, b_ref, after_ref, out_ref):
        total = a_ref[...].astype(F32) + b_ref[...].astype(F32)
        out_ref[...] = total.astype(BF16).reshape(out_ref.shape)

    def place(i):
        return owners[0]() * (1 - i) + owners[1]() * i

    block = pl.BlockSpec((2, 4, 1, 1, 32, 1024), lambda i: (0, 0, place(i), core_of(), 0, 0))
    return call(
        kernel,
        like((2, 2, 4, 32, 1024), BF16),
        grid=(2,),
        in_specs=[block, block, ANY],
        out_specs=pl.BlockSpec((1, 2, 4, 32, 1024), lambda i: (i, 0, 0, 0, 0)),
    )(mine.reshape(shape), got.reshape(shape), after)


def halves_sum(keep, got, after, flops=0):
    def kernel(a_ref, b_ref, after_ref, own_ref, send_ref):
        own_ref[...] = a_ref[0].astype(F32) + b_ref[0].astype(F32)
        send_ref[...] = (a_ref[1].astype(F32) + b_ref[1].astype(F32)).astype(BF16)

    block = keep.shape[1:]
    return call(
        kernel,
        [like(block, F32), like(block, BF16)],
        flops,
        in_specs=[VMEM] * 2 + [ANY],
        out_specs=[VMEM] * 2,
    )(keep, got, after)


def line_sum(own, got, after):
    def kernel(a_ref, b_ref, after_ref, send_ref, keep_ref):
        z_hi, core = z_hi_of(), core_of()
        owners = (first(z_hi, core), (z_hi + 2) % 4, z_hi, second(z_hi, core))
        for i, at in enumerate(owners):
            total = a_ref[:, at] + b_ref[:, at].astype(F32)
            (send_ref, keep_ref)[i // 2][i % 2] = total.astype(BF16)

    return call(
        kernel,
        [like((2, 2, 32, 1024), BF16)] * 2,
        in_specs=[VMEM] * 2 + [ANY],
        out_specs=[VMEM] * 2,
    )(own, got, after)


TILE = 256


def half_product(a, half, w, dtype, plus, after):
    rows, (depth, width) = a.shape[0], w.shape

    def kernel(a_ref, w_ref, *refs):
        total = jnp.dot(a_ref[...], w_ref[...], preferred_element_type=F32)
        for ref in refs[: len(plus)]:
            total = total + ref[...].astype(F32)
        refs[-1][...] = total.astype(dtype)

    column = lambda j: (0, j)
    return call(
        kernel,
        like((rows, width), dtype),
        grid=(width // TILE,),
        in_specs=[
            pl.BlockSpec((rows, depth), lambda j: (0, half())),
            pl.BlockSpec((depth, TILE), column),
        ]
        + [pl.BlockSpec((rows, TILE), column)] * len(plus)
        + [ANY],
        out_specs=pl.BlockSpec((rows, TILE), column),
    )(a, w, *plus, after)


def product(a, w, v, dtype, after):
    rows, depth, width = a.shape[0], w.shape[0], w.shape[1]

    def kernel(a_ref, w_ref, v_ref, after_ref, out_ref):
        for j in range(0, width, TILE):
            at = slice(j, j + TILE)
            total = jnp.dot(a_ref[:, :depth], w_ref[:, at], preferred_element_type=F32)
            total = total + jnp.dot(a_ref[:, depth:], v_ref[:, at], preferred_element_type=F32)
            out_ref[:, at] = total.astype(dtype)

    return call(
        kernel, like((rows, width), dtype), in_specs=[VMEM] * 3 + [ANY], out_specs=VMEM
    )(a, w, v, after)


def far_product(a, w, plus, after):
    rows, (depth, width) = a.shape[0], w.shape

    def kernel(a_ref, w_ref, plus_ref, after_ref, out_ref):
        value = a_ref[:, pl.ds(pl.multiple_of((1 - z_lo_of()) * depth, depth), depth)]
        for j in range(0, width, TILE):
            at = slice(j, j + TILE)
            total = jnp.dot(value, w_ref[:, at], preferred_element_type=F32)
            out_ref[:, at] = (total + plus_ref[:, at]).astype(BF16)

    return call(
        kernel, like((rows, width), BF16), in_specs=[VMEM] * 3 + [ANY], out_specs=VMEM
    )(a, w, plus, after)


def plus(own, got, dtype, after, flops=0):
    def kernel(own_ref, got_ref, after_ref, out_ref):
        out_ref[...] = (own_ref[...] + got_ref[...].astype(F32)).astype(dtype)

    return call(
        kernel, like(own.shape, dtype), flops, in_specs=[VMEM] * 2 + [ANY], out_specs=VMEM
    )(own, got, after)


def last_sum(own, got, scale):
    rows, width = own.shape
    cuts = 4
    tile = rows // cuts

    def kernel(own_ref, got_ref, scale_ref, out_ref, buf, sems):
        copies = []
        for i in range(cuts):
            part = slice(i * tile, (i + 1) * tile)
            total = own_ref[part] + got_ref[part].astype(F32)
            buf[part] = (total * scale_ref[part]).astype(BF16)
            copies.append(pltpu.make_async_copy(buf.at[part], out_ref.at[part], sems.at[i]))
            copies[-1].start()
        for copy in copies:
            copy.wait()

    return call(
        kernel,
        like(own.shape, BF16),
        in_specs=[VMEM] * 3,
        out_specs=ANY,
        scratch_shapes=[pltpu.VMEM((rows, width), BF16), DMA((cuts,))],
    )(own, got, scale)


def shards(local_fragment, anchor, momentum, next_weights, activations, norm_gain):
    replicas = lax.axis_size("rep")
    mine, fragment = next_weights[0], local_fragment[0]
    x_first = lambda v: move(v, lambda z, y, c, x, l: (z, y, c, first(x, c), l))
    x_second = lambda v: move(v, lambda z, y, c, x, l: (z, y, c, second(x, c), l))
    x_far = lambda v: move(v, lambda z, y, c, x, l: (z, y, c, (x + 2) % 4, l))
    y_first = lambda v: move(v, lambda z, y, c, x, l: (z, first(y, c), c, x, l))
    y_second = lambda v: move(v, lambda z, y, c, x, l: (z, second(y, c), c, x, l))
    z_first = lambda v: move(v, lambda z, y, c, x, l: (first(z, c), y, c, x, l))
    z_second = lambda v: move(v, lambda z, y, c, x, l: (second(z, c), y, c, x, l))

    other = move(mine, lambda z, y, c, x, l: (z, y, c, x, 1 - l))
    sibling = move(fragment, lambda z, y, c, x, l: (z, y, 1 - c, x, l))

    a_far = gained_block(activations, norm_gain, lambda: (x_of() + 2) % 4, norm_gain)
    far_a = x_far(a_far)
    a_first, a_second = gained(
        activations,
        norm_gain,
        [lambda: first(x_of(), core_of()), lambda: second(x_of(), core_of())],
        a_far,
    )
    first_a, second_a = x_first(a_first), x_second(a_second)
    scale = row_scale(activations, a_first)
    (own_a,) = gained(activations, norm_gain, [x_of], scale)

    send = pair_sum(
        fragment, sibling, [lambda: first(y_of(), core_of()), lambda: (y_of() + 2) % 4], own_a
    )
    got = y_first(send)
    keep = pair_sum(fragment, sibling, [y_of, lambda: second(y_of(), core_of())], send)
    own = half_product(own_a, lambda: 0, mine, F32, [], keep)
    far = half_product(far_a, z_lo_of, mine, F32, [], own)
    line, send = halves_sum(keep, got, far)
    got = y_second(send)

    far = far_product(far_a, other, far, send)
    via = x_first(far)
    send, keep = line_sum(line, got, far)
    got = z_first(send)
    near = product(first_a, mine, other, BF16, send)
    from_first = x_first(near)
    part = product(second_a, mine, other, F32, near)
    from_second = x_second(plus(part, via, BF16, part))
    total, send = halves_sum(keep, got, part, SLOW)
    got = z_second(send)
    own = half_product(own_a, lambda: 1, other, F32, [own], send)
    own = plus(own, from_first, F32, own, SLOW)

    total = total + got.astype(F32)
    pseudo = anchor - total / replicas
    new_momentum = 0.9 * momentum + pseudo
    new_anchor = anchor - 0.7 * (pseudo + 0.9 * new_momentum)
    result = last_sum(own, from_second, scale)
    return (new_anchor, new_momentum, result)


def solution(mesh):
    placed = (
        P("rep", None, "fsdp", None),
        P(None, ("fsdp", "rep"), None),
        P(None, ("fsdp", "rep"), None),
        P("rep", "fsdp", None),
        P(("rep", "fsdp"), None),
        P(),
    )
    return jax.shard_map(
        shards,
        mesh=mesh,
        in_specs=placed,
        out_specs=(
            P(None, ("fsdp", "rep"), None),
            P(None, ("fsdp", "rep"), None),
            P(("rep", "fsdp"), None),
        ),
        check_vma=False,
    )
```
